32 devices in a mesh: dp: 8 (over y, x, core), tensor: 4 (over z).
Axes of the slice: x: 2, y: 2, z: 4, core: 2. Of those that a mesh axis runs over, the one named last changes fastest.
Arguments:
- tokens: bfloat16 [1024, 4096], P('dp', 'tensor'), may hold values from -6 to 6
- cotangent: bfloat16 [1024, 4096], P('dp', 'tensor'), may hold values from -6 to 6
- expert_ids: int32 [1024, 8], P('dp'), may hold values from 0 to 15, all different within a row; in each aligned block of 128 rows (0 to 127, 128 to 255, ...) at most 96 rows name the same one
- route_weights: float32 [1024, 8], P('dp'), may hold values from 0.1 to 1
- w_gate: bfloat16 [16, 1536, 4096], P('dp', 'tensor'), may hold values from -0.09375 to 0.09375
- w_up: bfloat16 [16, 1536, 4096], P('dp', 'tensor'), may hold values from -0.09375 to 0.09375
Outputs:
- grad_down: bfloat16 [16, 1536, 4096], P('dp', 'tensor')
The draws below stay inside these ranges and needn't reach their ends.
Inputs may be any that keep to these rules, and one draw needn't show every extreme that they name: `expert_ids`: each row names 8 different experts. Among the 128 rows of one device no expert is named more than 96 times, a bound that some block reaches.
All inputs are finite; a program needn't handle non-finite values.
Results may differ from the reference program's by a relative error of at most 0.0058.
Values may be sent and summed in bfloat16 or wider, within the bound.
A program may use at most 128 MiB of HBM per device.

```python
import math
import jax
import jax.numpy as jnp
import numpy as np
from jax import lax

D = 4096
FF = 1536
TOPK = 8
TOK_DEV = 128
EXPERTS = 16
TOKENS = 1024
CAP = 96
N_DP = 8


def levels(rng, dims, cuts, smallest, top_value):
    loudness, own = 1.0, jax.random.fold_in(rng, 6)
    for axis_at, blocks in cuts:
        steps = jnp.exp(jax.random.uniform(jax.random.fold_in(own, axis_at), (blocks,), jnp.float32, smallest / len(cuts), top_value / len(cuts)))
        loudness = loudness * jnp.repeat(steps, dims[axis_at] // blocks).reshape([-1 if axis == axis_at else 1 for axis in range(len(dims))])
    return loudness


def assign_block(key, own, number, rows, number_of, top, most, lean):
    ranking = jax.random.permutation(key, number_of)
    crowded, usual = load_shares(number_of, rows * top, most, lean, True), load_shares(number_of, rows * top, most, lean, False)
    places = jnp.arange(number_of)

    def named(sizes, rotation):
        used = int((sizes > 0).sum())
        fixed = max(1, used // 4)
        passed = fixed + (places - fixed + rotation * (used - fixed)) % max(1, number_of - fixed)
        return jnp.zeros((number_of,), jnp.int32).at[ranking[jnp.where(places < fixed, places, passed)]].set(jnp.asarray(sizes, jnp.int32))

    sizes = jnp.where(number % 4 == 0, named(crowded, number // 4), named(usual, number - number // 4 - 1))
    mixed = jax.random.permutation(jax.random.fold_in(own, 3), number_of)
    donor, sink = mixed[0:number_of // 2 * 2:2], mixed[1:number_of // 2 * 2:2]
    slack = jnp.minimum(sizes[donor] - 1, most - sizes[sink]) // 2
    slack = jnp.where((donor == ranking[0]) | (sink == ranking[0]) | (sizes[sink] == 0), 0, jnp.maximum(slack, 0))
    passed = jax.random.randint(jax.random.fold_in(own, 4), (number_of // 2,), 0, 1 << 20) % (slack + 1)
    sizes = sizes.at[donor].add(-passed).at[sink].add(passed)
    items = jnp.searchsorted(jnp.cumsum(sizes), jnp.arange(rows * top), side="right").astype(jnp.int32)
    listing = items.reshape(top, rows).T
    listing = listing[jax.random.permutation(jax.random.fold_in(own, 1), rows)]
    rotation = jax.random.randint(jax.random.fold_in(own, 2), (rows, 1), 0, top)
    return jnp.take_along_axis(listing, (jnp.arange(top)[None, :] + rotation) % top, axis=1)


def load_shares(amount, total, bound, lean, full):
    portions = [(1 << 20) // math.isqrt(standing ** lean) + 1 for standing in range(1, amount + 1)]
    largest = bound if full else min(bound, max(-(-total // amount), total * portions[0] // sum(portions)))
    least = 1 if total - largest >= amount - 1 else 0
    counts, rest = [largest] + [least] * (amount - 1), total - largest - least * (amount - 1)
    while rest > 0:
        movable = [i for i in range(1, amount) if counts[i] < largest] or [i for i in range(1, amount) if counts[i] < bound]
        pool, budget = sum([portions[i] for i in movable]), rest
        for i in movable:
            extra = min(bound - counts[i], max(1, budget * portions[i] // pool), rest)
            counts[i] = counts[i] + extra
            rest = rest - extra
    return np.array(counts)


def noise(own_key, extent, deviation, limit, split=(), kind=jnp.bfloat16):
    drawn = jax.random.normal(own_key, extent, jnp.float32) * deviation
    if len(split) > 0:
        drawn = levels(own_key, extent, split, -0.22, 0.18) * drawn
    return jnp.clip(drawn, min=-limit, max=limit).astype(kind)


def setup_inputs(seed: int = 0) -> dict:
    seeds = jax.random.split(jax.random.key(seed), 7)
    tokens = noise(seeds[0], (TOKENS, D), 1.0, 6.0, ((0, 8), (1, 4)))
    cotangent = noise(seeds[1], (TOKENS, D), 1.0, 6.0, ((0, 8), (1, 4)))
    expert_ids_keys = jax.random.split(jax.random.fold_in(seeds[2], 1), TOKENS // TOK_DEV)
    expert_ids_turns = jax.random.permutation(jax.random.fold_in(seeds[2], 3), TOKENS // TOK_DEV)
    expert_ids = jax.vmap(lambda own, number: assign_block(jax.random.fold_in(seeds[2], 2), own, number, TOK_DEV, EXPERTS, TOPK, CAP, 2))(expert_ids_keys, expert_ids_turns).reshape((TOKENS, TOPK))
    route_weights = jnp.clip(0.1 + 0.9 * jax.random.uniform(seeds[3], (TOKENS, TOPK), jnp.float32) ** levels(seeds[3], (TOKENS, TOPK), ((0, 8),), -0.2, 0.2), 0.1, 1.0)
    w_gate = noise(seeds[4], (EXPERTS, FF, D), D ** -0.5, 0.09375, ((0, 8), (1, 4)))
    w_up = noise(seeds[5], (EXPERTS, FF, D), D ** -0.5, 0.09375, ((0, 8), (1, 4)))
    return {"tokens": tokens, "cotangent": cotangent, "expert_ids": expert_ids, "route_weights": route_weights, "w_gate": w_gate, "w_up": w_up}


def reference(tokens, cotangent, expert_ids, route_weights, w_gate, w_up):
    shares = route_weights / jnp.sum(route_weights, axis=1, keepdims=True)
    flat_shares = shares.reshape(-1)
    flat_ids = expert_ids.reshape(N_DP, TOK_DEV * TOPK).astype(jnp.int32)
    onehot = (flat_ids[:, :, None] == jnp.arange(EXPERTS).astype(jnp.int32)[None, None, :]).astype(jnp.int32)
    slot_index = jnp.sum((jnp.cumsum(onehot, axis=1) - 1) * onehot, axis=2).astype(jnp.int32)
    block_index = jnp.arange(N_DP).astype(jnp.int32)[:, None]
    target = (flat_ids * (N_DP * CAP) + block_index * CAP + slot_index).astype(jnp.int32)
    pair_index = jnp.arange(TOKENS * TOPK).astype(jnp.int32)
    slot_table = jnp.full((EXPERTS * N_DP * CAP,), -1, jnp.int32).at[target.reshape(-1)].set(pair_index)
    slot_table = slot_table.reshape(EXPERTS, N_DP * CAP)

    def per_expert(inputs_of):
        entries, gate_w, up_w = inputs_of
        is_live = entries >= 0
        safe_index = jnp.maximum(entries, 0)
        token_row = (safe_index // TOPK).astype(jnp.int32)
        routed = jnp.where(is_live[:, None], tokens[token_row], jnp.zeros((), tokens.dtype))
        weighting = jnp.where(is_live, flat_shares[safe_index], jnp.zeros((), flat_shares.dtype))
        scaled_rows = (weighting[:, None] * cotangent[token_row].astype(jnp.float32)).astype(jnp.bfloat16)
        gate_proj = jnp.dot(routed, gate_w.T, preferred_element_type=jnp.float32)
        up_proj = jnp.dot(routed, up_w.T, preferred_element_type=jnp.float32)
        hidden = (jax.nn.silu(gate_proj) * up_proj).astype(jnp.bfloat16)
        return jnp.dot(hidden.T, scaled_rows, preferred_element_type=jnp.float32).astype(jnp.bfloat16)

    return lax.map(per_expert, (slot_table, w_gate, w_up))
```

```python
import jax
import jax.numpy as jnp
from jax import lax
from jax.sharding import PartitionSpec as P


def shards(tokens, cotangent, expert_ids, route_weights, w_gate, w_up):
    dp_count = lax.axis_size("dp")
    exp_dev = w_gate.shape[0]
    experts = exp_dev * dp_count
    shares = route_weights / jnp.sum(route_weights, axis=1, keepdims=True)
    onehot = expert_ids[:, :, None] == jnp.arange(experts)[None, None, :]
    dense = jnp.sum(jnp.where(onehot, shares[:, :, None], 0.0), axis=1).T
    rows = lax.all_gather(lax.all_gather(tokens, "tensor", axis=1, tiled=True), "dp", axis=0, tiled=True)
    cots = lax.all_gather(lax.all_gather(cotangent, "tensor", axis=1, tiled=True), "dp", axis=0, tiled=True)
    mine = lax.all_to_all(dense, "dp", split_axis=0, concat_axis=1, tiled=True)
    gate = jnp.einsum("efd,rd->efr", w_gate, rows, preferred_element_type=jnp.float32)
    up = jnp.einsum("efd,rd->efr", w_up, rows, preferred_element_type=jnp.float32)
    hidden = (jax.nn.silu(gate) * up * mine[:, None, :]).astype(jnp.bfloat16)
    return jnp.einsum("efr,rd->efd", hidden, cots, preferred_element_type=jnp.float32).astype(jnp.bfloat16)


def solution(mesh):
    placed = (
        P("dp", "tensor"),
        P("dp", "tensor"),
        P("dp", None),
        P("dp", None),
        P("dp", "tensor", None),
        P("dp", "tensor", None),
    )
    return jax.shard_map(
        shards, mesh=mesh, in_specs=placed, out_specs=P("dp", "tensor", None), check_vma=False
    )
```

```python
import functools

import jax
import jax.numpy as jnp
from jax import lax
from jax.experimental import pallas as pl
from jax.experimental.pallas import tpu as pltpu
from jax.sharding import PartitionSpec as P

MESH = pl.DeviceIdType.MESH
VMEM_BUDGET = 58 * 1024 * 1024
UP, DOWN, TO_X, TO_Y, TO_SIB, X_TO_Y, X_SIB, Y_TO_X, Y_SIB, D_LO, D_HI = range(11)


def gather_kernel(
    sizes, tok, cot, ids, weights, w_gate, w_up, out,
    full, wv, acc, hid, obuf, share_all,
    send_sem, recv_sem, share_send, share_recv, load_sem, out_sem,
):
    dp_count, depth, rows, width, exp_dev, hidden = sizes
    experts = exp_dev * dp_count
    total = dp_count * rows
    held = exp_dev * hidden
    steps = 2 * depth
    me, z = lax.axis_index("dp"), lax.axis_index("tensor")
    core = lax.rem(me, 2)
    x = lax.rem(lax.div(me, 2), 2)
    y = lax.div(me, 4)
    sib = me + 1 - 2 * core
    xn = me + 2 - 4 * x
    yn = me + 4 - 8 * y
    dn = xn + 4 - 8 * y
    xs, ys, ds = xn + 1 - 2 * core, yn + 1 - 2 * core, dn + 1 - 2 * core

    def block(a, dp, zz, part=None):
        start, size = dp * rows, rows
        if part is not None:
            size = rows // 2
            start = start + part * size
        return full.at[
            a,
            pl.ds(pl.multiple_of(start, 16), size),
            pl.ds(pl.multiple_of(zz * width, 128), width),
        ]

    loads = [
        pltpu.make_async_copy(tok, block(0, me, z), load_sem.at[0]),
        pltpu.make_async_copy(cot, block(1, me, z), load_sem.at[1]),
        pltpu.make_async_copy(w_gate, wv.at[pl.ds(0, held)], load_sem.at[2]),
        pltpu.make_async_copy(w_up, wv.at[pl.ds(held, held)], load_sem.at[3]),
    ]
    for load in loads:
        load.start()

    barrier = pltpu.get_barrier_semaphore()
    for p in range(1, dp_count):
        pl.semaphore_signal(
            barrier, inc=1, device_id=(lax.rem(me + p, dp_count), z), device_id_type=MESH
        )

    @pl.when(z > 0)
    def _():
        pl.semaphore_signal(barrier, inc=1, device_id=(me, z - 1), device_id_type=MESH)

    @pl.when(z < depth - 1)
    def _():
        pl.semaphore_signal(barrier, inc=1, device_id=(me, z + 1), device_id_type=MESH)

    raw = weights[...]
    share = raw / jnp.sum(raw, axis=0, keepdims=True)
    named = ids[...]
    lines = [
        jnp.sum(jnp.where(named == e, share, 0.0), axis=0, keepdims=True) for e in range(experts)
    ]
    share_all[me] = jnp.concatenate(lines, axis=0)

    ends = jnp.where(z > 0, 1, 0) + jnp.where(z < depth - 1, 1, 0)
    pl.semaphore_wait(barrier, dp_count - 1 + ends)

    def place(k):
        a = lax.div(k, depth)
        s = k - a * depth
        m = jnp.minimum(z, depth - 1 - z)
        near = jnp.where(lax.rem(s, 2) == 1, z - lax.div(s + 1, 2), z + lax.div(s, 2))
        far = jnp.where(z == m, s, depth - 1 - s)
        zz = jnp.where(s <= 2 * m, near, far)
        return a, zz, a * depth + zz

    def remote(ref, r, kind, dp, zt, at=None):
        return pltpu.make_async_remote_copy(
            src_ref=ref,
            dst_ref=ref,
            send_sem=send_sem.at[r, kind],
            recv_sem=recv_sem.at[r, kind if at is None else at],
            device_id=(dp, zt),
            device_id_type=MESH,
        )

    def share_copy(p, dst):
        return pltpu.make_async_remote_copy(
            src_ref=share_all.at[me],
            dst_ref=share_all.at[me],
            send_sem=share_send.at[p],
            recv_sem=share_recv.at[p],
            device_id=(dst, z),
            device_id_type=MESH,
        )

    def line_block(k):
        a, zz, r = place(k)
        own = block(a, me, zz)

        @pl.when(zz != z)
        def _():
            remote(own, r, UP, me, z).wait_recv()

        @pl.when((zz <= z) & (z < depth - 1))
        def _():
            remote(own, r, UP, me, z + 1).start()

        @pl.when((zz >= z) & (z > 0))
        def _():
            remote(own, r, DOWN, me, z - 1, UP).start()

        remote(own, r, TO_X, xn, z).start()
        remote(own, r, TO_Y, yn, z).start()
        remote(own, r, TO_SIB, sib, z).start()

    def neighbour_blocks(k):
        a, zz, r = place(k)
        remote(block(a, xn, zz), r, TO_X, xn, z).wait_recv()
        remote(block(a, xn, zz, 0), r, X_TO_Y, yn, z).start()
        remote(block(a, xn, zz), r, X_SIB, sib, z).start()
        remote(block(a, yn, zz), r, TO_Y, yn, z).wait_recv()
        remote(block(a, yn, zz, 1), r, Y_TO_X, xn, z).start()
        remote(block(a, yn, zz), r, Y_SIB, sib, z).start()

    def diagonal_blocks(k):
        a, zz, r = place(k)
        remote(block(a, dn, zz, 0), r, X_TO_Y, yn, z).wait_recv()
        remote(block(a, dn, zz, 0), r, D_LO, sib, z).start()
        remote(block(a, dn, zz, 1), r, Y_TO_X, xn, z).wait_recv()
        remote(block(a, dn, zz, 1), r, D_HI, sib, z).start()

    def sibling_blocks(k):
        a, zz, r = place(k)
        remote(block(a, sib, zz), r, TO_SIB, sib, z).wait_recv()
        remote(block(a, xs, zz), r, X_SIB, sib, z).wait_recv()
        remote(block(a, ys, zz), r, Y_SIB, sib, z).wait_recv()
        remote(block(a, ds, zz, 0), r, D_LO, sib, z).wait_recv()
        remote(block(a, ds, zz, 1), r, D_HI, sib, z).wait_recv()

    def sent(k):
        a, zz, r = place(k)
        own = block(a, me, zz)

        @pl.when((zz <= z) & (z < depth - 1))
        def _():
            remote(own, r, UP, me, z + 1).wait_send()

        @pl.when((zz >= z) & (z > 0))
        def _():
            remote(own, r, DOWN, me, z - 1, UP).wait_send()

        remote(own, r, TO_X, xn, z).wait_send()
        remote(own, r, TO_Y, yn, z).wait_send()
        remote(own, r, TO_SIB, sib, z).wait_send()
        remote(block(a, xn, zz, 0), r, X_TO_Y, yn, z).wait_send()
        remote(block(a, xn, zz), r, X_SIB, sib, z).wait_send()
        remote(block(a, yn, zz, 1), r, Y_TO_X, xn, z).wait_send()
        remote(block(a, yn, zz), r, Y_SIB, sib, z).wait_send()
        remote(block(a, dn, zz, 0), r, D_LO, sib, z).wait_send()
        remote(block(a, dn, zz, 1), r, D_HI, sib, z).wait_send()

    tile = 256

    def project(k):
        _, zz, _ = place(k)
        cols = pl.ds(pl.multiple_of(zz * width, 128), width)
        for g in range(2):
            @pl.loop(0, total // tile)
            def _(i):
                at = pl.ds(pl.multiple_of(i * tile, tile), tile)
                part = lax.dot_general(
                    wv[pl.ds(g * held, held), cols],
                    full[0, at, cols],
                    (((1,), (1,)), ((), ())),
                    preferred_element_type=jnp.float32,
                )

                @pl.when(k == 0)
                def _():
                    acc[pl.ds(g * held, held), at] = part

                @pl.when(k > 0)
                def _():
                    acc[pl.ds(g * held, held), at] += part

    def activate():
        for p in range(1, dp_count):
            src = lax.rem(me + dp_count - p, dp_count)
            pltpu.make_async_remote_copy(
                src_ref=share_all.at[src],
                dst_ref=share_all.at[src],
                send_sem=share_send.at[p],
                recv_sem=share_recv.at[p],
                device_id=(src, z),
                device_id_type=MESH,
            ).wait_recv()

        @pl.loop(0, dp_count)
        def _(p):
            at = pl.ds(pl.multiple_of(p * rows, 128), rows)
            for e in range(exp_dev):
                gate = acc[pl.ds(e * hidden, hidden), at]
                up = acc[pl.ds(held + e * hidden, hidden), at]
                line = share_all[p, pl.ds(me * exp_dev + e, 1), :]
                value = gate / (1.0 + jnp.exp(-gate)) * up * line
                hid[pl.ds(e * hidden, hidden), at] = value.astype(hid.dtype)

    def store(k):
        _, zz, _ = place(k)
        cols = pl.ds(pl.multiple_of(zz * width, 128), width)
        return pltpu.make_async_copy(obuf.at[:, cols], out.at[:, cols], out_sem.at[zz])

    def down(k):
        _, zz, _ = place(k)

        @pl.loop(0, width // tile)
        def _(i):
            at = pl.ds(pl.multiple_of(zz * width + i * tile, tile), tile)
            obuf[:, at] = jnp.dot(
                hid[...], full[1, :, at], preferred_element_type=jnp.float32
            ).astype(obuf.dtype)

        store(k).start()

    loads[0].wait()
    loads[1].wait()
    line_block(0)
    for p in range(1, dp_count):
        share_copy(p, lax.rem(me + p, dp_count)).start()
    line_block(1)
    neighbour_blocks(0)
    loads[2].wait()
    loads[3].wait()

    @pl.loop(0, steps)
    def _(k):
        @pl.when(k + 2 < steps)
        def _():
            line_block(k + 2)

        @pl.when(k + 1 < steps)
        def _():
            neighbour_blocks(k + 1)

        diagonal_blocks(k)
        sibling_blocks(k)

        @pl.when(k < depth)
        def _():
            project(k)

        @pl.when(k == depth - 1)
        def _():
            activate()

        @pl.when(k >= depth)
        def _():
            down(k)

    @pl.loop(0, steps)
    def _(k):
        sent(k)

    for p in range(1, dp_count):
        share_copy(p, lax.rem(me + p, dp_count)).wait_send()

    @pl.loop(depth, steps)
    def _(k):
        store(k).wait()


def scratch_bytes(dp_count, depth, rows, width, exp_dev, hidden):
    total, model, held = dp_count * rows, depth * width, exp_dev * hidden
    return 4 * total * model + 4 * held * model + 8 * held * total + 2 * held * (total + model)


def gather_plan(sizes, tokens, cotangent, expert_ids, route_weights, w_gate, w_up):
    dp_count, depth, rows, width, exp_dev, hidden = sizes
    total, model, held = dp_count * rows, depth * width, exp_dev * hidden
    experts = exp_dev * dp_count
    steps = 2 * depth
    hbm = pl.BlockSpec(memory_space=pl.ANY)
    vmem = pl.BlockSpec(memory_space=pltpu.VMEM)
    grad = pl.pallas_call(
        functools.partial(gather_kernel, sizes),
        out_shape=jax.ShapeDtypeStruct((held, model), jnp.bfloat16),
        in_specs=[hbm, hbm, vmem, vmem, hbm, hbm],
        out_specs=hbm,
        scratch_shapes=[
            pltpu.VMEM((2, total, model), jnp.bfloat16),
            pltpu.VMEM((2 * held, model), jnp.bfloat16),
            pltpu.VMEM((2 * held, total), jnp.float32),
            pltpu.VMEM((held, total), jnp.bfloat16),
            pltpu.VMEM((held, model), jnp.bfloat16),
            pltpu.VMEM((dp_count, experts, rows), jnp.float32),
            pltpu.SemaphoreType.DMA((steps, 11)),
            pltpu.SemaphoreType.DMA((steps, 11)),
            pltpu.SemaphoreType.DMA((dp_count,)),
            pltpu.SemaphoreType.DMA((dp_count,)),
            pltpu.SemaphoreType.DMA((4,)),
            pltpu.SemaphoreType.DMA((depth,)),
        ],
        compiler_params=pltpu.CompilerParams(
            collective_id=0, has_side_effects=True, vmem_limit_bytes=VMEM_BUDGET
        ),
        cost_estimate=pl.CostEstimate(
            flops=6 * held * total * model,
            bytes_accessed=6 * held * model + 4 * rows * width,
            transcendentals=held * total,
        ),
    )(
        tokens,
        cotangent,
        expert_ids.T,
        route_weights.T,
        w_gate.reshape(held, model),
        w_up.reshape(held, model),
    )
    return grad.reshape(exp_dev, hidden, model)


def build_table(flat_ids, first_expert, held_count, block_count, capacity):
    local_expert = flat_ids - first_expert
    inside = (local_expert >= 0) & (local_expert < held_count)
    onehot = (local_expert[:, :, None] == jnp.arange(held_count)[None, None, :]).astype(jnp.int32)
    slot_index = jnp.sum((jnp.cumsum(onehot, axis=1) - 1) * onehot, axis=2)
    block_index = jnp.arange(block_count)[:, None]
    target = local_expert * (block_count * capacity) + block_index * capacity + slot_index
    target = jnp.where(inside, target, held_count * block_count * capacity)
    pair_index = jnp.arange(flat_ids.shape[0] * flat_ids.shape[1])
    empty_table = jnp.full((held_count * block_count * capacity,), -1, jnp.int32)
    return empty_table.at[target.reshape(-1)].set(pair_index, mode="drop")


def pick_rows(slot_table, token_rows, cot_rows, flat_shares, top_count):
    is_live = slot_table >= 0
    safe_index = jnp.maximum(slot_table, 0)
    token_row = safe_index // top_count
    routed = jnp.where(is_live[:, None], token_rows[token_row], jnp.zeros((), token_rows.dtype))
    weighting = jnp.where(is_live, flat_shares[safe_index], 0.0)
    scaled_rows = (weighting[:, None] * cot_rows[token_row].astype(jnp.float32)).astype(
        jnp.bfloat16
    )
    return (routed, scaled_rows)


def routed_plan(tokens, cotangent, expert_ids, route_weights, w_gate, w_up):
    dp_count = lax.axis_size("dp")
    exp_dev = w_gate.shape[0]
    experts = exp_dev * dp_count
    tok_rows, width_local = tokens.shape
    top_count = expert_ids.shape[1]
    capacity = 3 * tok_rows * top_count // (2 * experts)
    shares = route_weights / jnp.sum(route_weights, axis=1, keepdims=True)
    slot_table = build_table(expert_ids.reshape(1, tok_rows * top_count), 0, experts, 1, capacity)
    routed, scaled_rows = pick_rows(slot_table, tokens, cotangent, shares.reshape(-1), top_count)
    send_rows = routed.reshape(experts, capacity, width_local)
    send_cot = scaled_rows.reshape(experts, capacity, width_local)
    wide_rows = lax.all_gather(send_rows, "tensor", axis=2, tiled=True)
    received, cot_recv = (
        lax.all_to_all(wide_rows, "dp", split_axis=0, concat_axis=1, tiled=True),
        lax.all_to_all(send_cot, "dp", split_axis=0, concat_axis=1, tiled=True),
    )
    gate_proj = jnp.einsum("erd,efd->erf", received, w_gate, preferred_element_type=jnp.float32)
    up_proj = jnp.einsum("erd,efd->erf", received, w_up, preferred_element_type=jnp.float32)
    hidden = (jax.nn.silu(gate_proj) * up_proj).astype(jnp.bfloat16)
    return jnp.einsum(
        "erf,erd->efd",
        hidden,
        lax.all_gather(cot_recv, "tensor", axis=2, tiled=True),
        preferred_element_type=jnp.float32,
    ).astype(jnp.bfloat16)


def shards(tokens, cotangent, expert_ids, route_weights, w_gate, w_up):
    dp_count, depth = lax.axis_size("dp"), lax.axis_size("tensor")
    sizes = (dp_count, depth) + tokens.shape + w_gate.shape[:2]
    if dp_count == 8 and scratch_bytes(*sizes) < VMEM_BUDGET * 9 // 10:
        return gather_plan(sizes, tokens, cotangent, expert_ids, route_weights, w_gate, w_up)
    return routed_plan(tokens, cotangent, expert_ids, route_weights, w_gate, w_up)


def solution(mesh):
    placed = (
        P("dp", "tensor"),
        P("dp", "tensor"),
        P("dp", None),
        P("dp", None),
        P("dp", "tensor", None),
        P("dp", "tensor", None),
    )
    return jax.shard_map(
        shards, mesh=mesh, in_specs=placed, out_specs=P("dp", "tensor", None), check_vma=False
    )
```

```python
import functools

import jax
import jax.numpy as jnp
from jax import lax
from jax.experimental import pallas as pl
from jax.experimental.pallas import tpu as pltpu
from jax.sharding import PartitionSpec as P

MESH = pl.DeviceIdType.MESH
VMEM_BUDGET = 58 * 1024 * 1024
UP, DOWN, TO_X, TO_Y, TO_SIB, X_TO_Y, X_SIB, Y_TO_X, Y_SIB, D_LO, D_HI, DZ_UP, DZ_DOWN = range(13)
KINDS = 13


def gather_kernel(
    sizes, tok, cot, ids, weights, w_gate, w_up, out,
    full, wv, acc, hid, obuf, share_all,
    send_sem, recv_sem, share_send, share_recv, load_sem, out_sem,
):
    dp_count, depth, rows, width, exp_dev, hidden = sizes
    experts = exp_dev * dp_count
    total = dp_count * rows
    held = exp_dev * hidden
    steps = 2 * depth
    me, z = lax.axis_index("dp"), lax.axis_index("tensor")
    core = lax.rem(me, 2)
    x = lax.rem(lax.div(me, 2), 2)
    y = lax.div(me, 4)
    sib = me + 1 - 2 * core
    xn = me + 2 - 4 * x
    yn = me + 4 - 8 * y
    dn = xn + 4 - 8 * y
    xs, ys, ds = xn + 1 - 2 * core, yn + 1 - 2 * core, dn + 1 - 2 * core

    half, quarter = rows // 2, rows // 4
    lo, hi = (0, half), (half, half)
    lo_first, lo_second = (0, quarter), (quarter, quarter)

    def block(a, dp, zz, part=None):
        start, size = dp * rows, rows
        if part is not None:
            start, size = start + part[0], part[1]
        return full.at[
            a,
            pl.ds(pl.multiple_of(start, 16), size),
            pl.ds(pl.multiple_of(zz * width, 128), width),
        ]

    loads = [
        pltpu.make_async_copy(tok, block(0, me, z), load_sem.at[0]),
        pltpu.make_async_copy(cot, block(1, me, z), load_sem.at[1]),
        pltpu.make_async_copy(w_gate, wv.at[pl.ds(0, held)], load_sem.at[2]),
        pltpu.make_async_copy(w_up, wv.at[pl.ds(held, held)], load_sem.at[3]),
    ]
    for load in loads:
        load.start()

    barrier = pltpu.get_barrier_semaphore()
    for p in range(1, dp_count):
        pl.semaphore_signal(
            barrier, inc=1, device_id=(lax.rem(me + p, dp_count), z), device_id_type=MESH
        )

    @pl.when(z > 0)
    def _():
        pl.semaphore_signal(barrier, inc=1, device_id=(me, z - 1), device_id_type=MESH)

    @pl.when(z < depth - 1)
    def _():
        pl.semaphore_signal(barrier, inc=1, device_id=(me, z + 1), device_id_type=MESH)

    raw = weights[...]
    share = raw / jnp.sum(raw, axis=0, keepdims=True)
    named = ids[...]
    lines = [
        jnp.sum(jnp.where(named == e, share, 0.0), axis=0, keepdims=True) for e in range(experts)
    ]
    share_all[me] = jnp.concatenate(lines, axis=0)

    ends = jnp.where(z > 0, 1, 0) + jnp.where(z < depth - 1, 1, 0)
    pl.semaphore_wait(barrier, dp_count - 1 + ends)

    def place(k):
        a = lax.div(k, depth)
        s = k - a * depth
        m = jnp.minimum(z, depth - 1 - z)
        near = jnp.where(lax.rem(s, 2) == 1, z - lax.div(s + 1, 2), z + lax.div(s, 2))
        far = jnp.where(z == m, s, depth - 1 - s)
        zz = jnp.where(s <= 2 * m, near, far)
        return a, zz, a * depth + zz

    def remote(ref, r, kind, dp, zt, at=None):
        return pltpu.make_async_remote_copy(
            src_ref=ref,
            dst_ref=ref,
            send_sem=send_sem.at[r, kind],
            recv_sem=recv_sem.at[r, kind if at is None else at],
            device_id=(dp, zt),
            device_id_type=MESH,
        )

    def share_copy(p, dst):
        return pltpu.make_async_remote_copy(
            src_ref=share_all.at[me],
            dst_ref=share_all.at[me],
            send_sem=share_send.at[p],
            recv_sem=share_recv.at[p],
            device_id=(dst, z),
            device_id_type=MESH,
        )

    def line_block(k):
        a, zz, r = place(k)
        own = block(a, me, zz)

        @pl.when(zz != z)
        def _():
            remote(own, r, UP, me, z).wait_recv()

        @pl.when((zz <= z) & (z < depth - 1))
        def _():
            remote(own, r, UP, me, z + 1).start()

        @pl.when((zz >= z) & (z > 0))
        def _():
            remote(own, r, DOWN, me, z - 1, UP).start()

        remote(own, r, TO_X, xn, z).start()
        remote(own, r, TO_Y, yn, z).start()
        remote(own, r, TO_SIB, sib, z).start()

    def corner_start(a, zz, r, dp, kind, dst, near_part, far_part):
        @pl.when(zz == z)
        def _():
            remote(block(a, dp, zz, near_part), r, kind, dst, z).start()

        @pl.when(zz != z)
        def _():
            remote(block(a, dp, zz, far_part), r, kind, dst, z).start()

    def neighbour_blocks(k):
        a, zz, r = place(k)
        remote(block(a, xn, zz), r, TO_X, xn, z).wait_recv()
        corner_start(a, zz, r, xn, X_TO_Y, yn, lo, lo_first)
        remote(block(a, xn, zz), r, X_SIB, sib, z).start()
        remote(block(a, yn, zz), r, TO_Y, yn, z).wait_recv()
        corner_start(a, zz, r, yn, Y_TO_X, xn, hi, lo_second)
        remote(block(a, yn, zz), r, Y_SIB, sib, z).start()

    def diagonal_blocks(k):
        a, zz, r = place(k)

        @pl.when(zz == z)
        def _():
            remote(block(a, dn, zz, lo), r, X_TO_Y, yn, z).wait_recv()
            remote(block(a, dn, zz, hi), r, Y_TO_X, xn, z).wait_recv()

        @pl.when(zz != z)
        def _():
            remote(block(a, dn, zz, hi), r, DZ_UP, me, z).wait_recv()

        corner = block(a, dn, zz, hi)

        @pl.when((zz <= z) & (z < depth - 1))
        def _():
            remote(corner, r, DZ_UP, me, z + 1).start()

        @pl.when((zz >= z) & (z > 0))
        def _():
            remote(corner, r, DZ_DOWN, me, z - 1, DZ_UP).start()

        remote(corner, r, D_HI, sib, z).start()

        @pl.when(zz != z)
        def _():
            remote(block(a, dn, zz, lo_first), r, X_TO_Y, yn, z).wait_recv()
            remote(block(a, dn, zz, lo_second), r, Y_TO_X, xn, z).wait_recv()

        remote(block(a, dn, zz, lo), r, D_LO, sib, z).start()

    def sibling_blocks(k):
        a, zz, r = place(k)
        remote(block(a, sib, zz), r, TO_SIB, sib, z).wait_recv()
        remote(block(a, xs, zz), r, X_SIB, sib, z).wait_recv()
        remote(block(a, ys, zz), r, Y_SIB, sib, z).wait_recv()
        remote(block(a, ds, zz, lo), r, D_LO, sib, z).wait_recv()
        remote(block(a, ds, zz, hi), r, D_HI, sib, z).wait_recv()

    def sent(k):
        a, zz, r = place(k)
        own = block(a, me, zz)

        @pl.when((zz <= z) & (z < depth - 1))
        def _():
            remote(own, r, UP, me, z + 1).wait_send()

        @pl.when((zz >= z) & (z > 0))
        def _():
            remote(own, r, DOWN, me, z - 1, UP).wait_send()

        remote(own, r, TO_X, xn, z).wait_send()
        remote(own, r, TO_Y, yn, z).wait_send()
        remote(own, r, TO_SIB, sib, z).wait_send()
        remote(block(a, xn, zz), r, X_SIB, sib, z).wait_send()
        remote(block(a, yn, zz), r, Y_SIB, sib, z).wait_send()
        remote(block(a, dn, zz, lo), r, D_LO, sib, z).wait_send()
        corner = block(a, dn, zz, hi)
        remote(corner, r, D_HI, sib, z).wait_send()

        @pl.when(zz == z)
        def _():
            remote(block(a, xn, zz, lo), r, X_TO_Y, yn, z).wait_send()
            remote(block(a, yn, zz, hi), r, Y_TO_X, xn, z).wait_send()

        @pl.when(zz != z)
        def _():
            remote(block(a, xn, zz, lo_first), r, X_TO_Y, yn, z).wait_send()
            remote(block(a, yn, zz, lo_second), r, Y_TO_X, xn, z).wait_send()

        @pl.when((zz <= z) & (z < depth - 1))
        def _():
            remote(corner, r, DZ_UP, me, z + 1).wait_send()

        @pl.when((zz >= z) & (z > 0))
        def _():
            remote(corner, r, DZ_DOWN, me, z - 1, DZ_UP).wait_send()

    tile = 256

    def project(k):
        _, zz, _ = place(k)
        cols = pl.ds(pl.multiple_of(zz * width, 128), width)
        for g in range(2):
            @pl.loop(0, total // tile)
            def _(i):
                at = pl.ds(pl.multiple_of(i * tile, tile), tile)
                part = lax.dot_general(
                    wv[pl.ds(g * held, held), cols],
                    full[0, at, cols],
                    (((1,), (1,)), ((), ())),
                    preferred_element_type=jnp.float32,
                )

                @pl.when(k == 0)
                def _():
                    acc[pl.ds(g * held, held), at] = part

                @pl.when(k > 0)
                def _():
                    acc[pl.ds(g * held, held), at] += part

    def activate():
        for p in range(1, dp_count):
            src = lax.rem(me + dp_count - p, dp_count)
            pltpu.make_async_remote_copy(
                src_ref=share_all.at[src],
                dst_ref=share_all.at[src],
                send_sem=share_send.at[p],
                recv_sem=share_recv.at[p],
                device_id=(src, z),
                device_id_type=MESH,
            ).wait_recv()

        @pl.loop(0, dp_count)
        def _(p):
            at = pl.ds(pl.multiple_of(p * rows, 128), rows)
            for e in range(exp_dev):
                gate = acc[pl.ds(e * hidden, hidden), at]
                up = acc[pl.ds(held + e * hidden, hidden), at]
                line = share_all[p, pl.ds(me * exp_dev + e, 1), :]
                value = gate / (1.0 + jnp.exp(-gate)) * up * line
                hid[pl.ds(e * hidden, hidden), at] = value.astype(hid.dtype)

    def store(k):
        _, zz, _ = place(k)
        cols = pl.ds(pl.multiple_of(zz * width, 128), width)
        return pltpu.make_async_copy(obuf.at[:, cols], out.at[:, cols], out_sem.at[zz])

    def down(k):
        _, zz, _ = place(k)

        @pl.loop(0, width // tile)
        def _(i):
            at = pl.ds(pl.multiple_of(zz * width + i * tile, tile), tile)
            obuf[:, at] = jnp.dot(
                hid[...], full[1, :, at], preferred_element_type=jnp.float32
            ).astype(obuf.dtype)

        store(k).start()

    loads[0].wait()
    loads[1].wait()
    line_block(0)
    for p in range(1, dp_count):
        share_copy(p, lax.rem(me + p, dp_count)).start()
    line_block(1)
    neighbour_blocks(0)
    line_block(2)
    neighbour_blocks(1)
    diagonal_blocks(0)
    loads[2].wait()
    loads[3].wait()

    @pl.loop(0, steps)
    def _(k):
        @pl.when(k + 3 < steps)
        def _():
            line_block(k + 3)

        @pl.when(k + 2 < steps)
        def _():
            neighbour_blocks(k + 2)

        @pl.when(k + 1 < steps)
        def _():
            diagonal_blocks(k + 1)

        sibling_blocks(k)

        @pl.when(k < depth)
        def _():
            project(k)

        @pl.when(k == depth - 1)
        def _():
            activate()

        @pl.when(k >= depth)
        def _():
            down(k)

    @pl.loop(0, steps)
    def _(k):
        sent(k)

    for p in range(1, dp_count):
        share_copy(p, lax.rem(me + p, dp_count)).wait_send()

    @pl.loop(depth, steps)
    def _(k):
        store(k).wait()


def scratch_bytes(dp_count, depth, rows, width, exp_dev, hidden):
    total, model, held = dp_count * rows, depth * width, exp_dev * hidden
    return 4 * total * model + 4 * held * model + 8 * held * total + 2 * held * (total + model)


def gather_plan(sizes, tokens, cotangent, expert_ids, route_weights, w_gate, w_up):
    dp_count, depth, rows, width, exp_dev, hidden = sizes
    total, model, held = dp_count * rows, depth * width, exp_dev * hidden
    experts = exp_dev * dp_count
    steps = 2 * depth
    hbm = pl.BlockSpec(memory_space=pl.ANY)
    vmem = pl.BlockSpec(memory_space=pltpu.VMEM)
    grad = pl.pallas_call(
        functools.partial(gather_kernel, sizes),
        out_shape=jax.ShapeDtypeStruct((held, model), jnp.bfloat16),
        in_specs=[hbm, hbm, vmem, vmem, hbm, hbm],
        out_specs=hbm,
        scratch_shapes=[
            pltpu.VMEM((2, total, model), jnp.bfloat16),
            pltpu.VMEM((2 * held, model), jnp.bfloat16),
            pltpu.VMEM((2 * held, total), jnp.float32),
            pltpu.VMEM((held, total), jnp.bfloat16),
            pltpu.VMEM((held, model), jnp.bfloat16),
            pltpu.VMEM((dp_count, experts, rows), jnp.float32),
            pltpu.SemaphoreType.DMA((steps, KINDS)),
            pltpu.SemaphoreType.DMA((steps, KINDS)),
            pltpu.SemaphoreType.DMA((dp_count,)),
            pltpu.SemaphoreType.DMA((dp_count,)),
            pltpu.SemaphoreType.DMA((4,)),
            pltpu.SemaphoreType.DMA((depth,)),
        ],
        compiler_params=pltpu.CompilerParams(
            collective_id=0, has_side_effects=True, vmem_limit_bytes=VMEM_BUDGET
        ),
        cost_estimate=pl.CostEstimate(
            flops=6 * held * total * model,
            bytes_accessed=6 * held * model + 4 * rows * width,
            transcendentals=held * total,
        ),
    )(
        tokens,
        cotangent,
        expert_ids.T,
        route_weights.T,
        w_gate.reshape(held, model),
        w_up.reshape(held, model),
    )
    return grad.reshape(exp_dev, hidden, model)


def build_table(flat_ids, first_expert, held_count, block_count, capacity):
    local_expert = flat_ids - first_expert
    inside = (local_expert >= 0) & (local_expert < held_count)
    onehot = (local_expert[:, :, None] == jnp.arange(held_count)[None, None, :]).astype(jnp.int32)
    slot_index = jnp.sum((jnp.cumsum(onehot, axis=1) - 1) * onehot, axis=2)
    block_index = jnp.arange(block_count)[:, None]
    target = local_expert * (block_count * capacity) + block_index * capacity + slot_index
    target = jnp.where(inside, target, held_count * block_count * capacity)
    pair_index = jnp.arange(flat_ids.shape[0] * flat_ids.shape[1])
    empty_table = jnp.full((held_count * block_count * capacity,), -1, jnp.int32)
    return empty_table.at[target.reshape(-1)].set(pair_index, mode="drop")


def pick_rows(slot_table, token_rows, cot_rows, flat_shares, top_count):
    is_live = slot_table >= 0
    safe_index = jnp.maximum(slot_table, 0)
    token_row = safe_index // top_count
    routed = jnp.where(is_live[:, None], token_rows[token_row], jnp.zeros((), token_rows.dtype))
    weighting = jnp.where(is_live, flat_shares[safe_index], 0.0)
    scaled_rows = (weighting[:, None] * cot_rows[token_row].astype(jnp.float32)).astype(
        jnp.bfloat16
    )
    return (routed, scaled_rows)


def routed_plan(tokens, cotangent, expert_ids, route_weights, w_gate, w_up):
    dp_count = lax.axis_size("dp")
    exp_dev = w_gate.shape[0]
    experts = exp_dev * dp_count
    tok_rows, width_local = tokens.shape
    top_count = expert_ids.shape[1]
    capacity = 3 * tok_rows * top_count // (2 * experts)
    shares = route_weights / jnp.sum(route_weights, axis=1, keepdims=True)
    slot_table = build_table(expert_ids.reshape(1, tok_rows * top_count), 0, experts, 1, capacity)
    routed, scaled_rows = pick_rows(slot_table, tokens, cotangent, shares.reshape(-1), top_count)
    send_rows = routed.reshape(experts, capacity, width_local)
    send_cot = scaled_rows.reshape(experts, capacity, width_local)
    wide_rows = lax.all_gather(send_rows, "tensor", axis=2, tiled=True)
    received, cot_recv = (
        lax.all_to_all(wide_rows, "dp", split_axis=0, concat_axis=1, tiled=True),
        lax.all_to_all(send_cot, "dp", split_axis=0, concat_axis=1, tiled=True),
    )
    gate_proj = jnp.einsum("erd,efd->erf", received, w_gate, preferred_element_type=jnp.float32)
    up_proj = jnp.einsum("erd,efd->erf", received, w_up, preferred_element_type=jnp.float32)
    hidden = (jax.nn.silu(gate_proj) * up_proj).astype(jnp.bfloat16)
    return jnp.einsum(
        "erf,erd->efd",
        hidden,
        lax.all_gather(cot_recv, "tensor", axis=2, tiled=True),
        preferred_element_type=jnp.float32,
    ).astype(jnp.bfloat16)


def shards(tokens, cotangent, expert_ids, route_weights, w_gate, w_up):
    dp_count, depth = lax.axis_size("dp"), lax.axis_size("tensor")
    sizes = (dp_count, depth) + tokens.shape + w_gate.shape[:2]
    if dp_count == 8 and scratch_bytes(*sizes) < VMEM_BUDGET * 9 // 10:
        return gather_plan(sizes, tokens, cotangent, expert_ids, route_weights, w_gate, w_up)
    return routed_plan(tokens, cotangent, expert_ids, route_weights, w_gate, w_up)


def solution(mesh):
    placed = (
        P("dp", "tensor"),
        P("dp", "tensor"),
        P("dp", None),
        P("dp", None),
        P("dp", "tensor", None),
        P("dp", "tensor", None),
    )
    return jax.shard_map(
        shards, mesh=mesh, in_specs=placed, out_specs=P("dp", "tensor", None), check_vma=False
    )
```

```python
import functools
import math

import jax
import jax.numpy as jnp
from jax import lax
from jax.experimental import pallas as pl
from jax.experimental.pallas import tpu as pltpu
from jax.sharding import PartitionSpec as P

MESH = pl.DeviceIdType.MESH
VMEM_BUDGET = 58 * 1024 * 1024
UP, DOWN, TO_X, TO_Y, TO_SIB, X_TO_Y, X_SIB, Y_TO_X, Y_SIB, D_LO, D_HI, DZ_UP, DZ_DOWN = range(13)
KINDS = 13


def gather_kernel(
    sizes, tok, cot, ids, weights, w_gate, w_up, out,
    full, wv, acc, hid, obuf, share_all,
    send_sem, recv_sem, share_send, share_recv, load_sem, out_sem,
):
    dp_count, depth, rows, width, exp_dev, hidden = sizes
    experts = exp_dev * dp_count
    total = dp_count * rows
    held = exp_dev * hidden
    steps = 2 * depth
    me, z = lax.axis_index("dp"), lax.axis_index("tensor")
    core = lax.rem(me, 2)
    x = lax.rem(lax.div(me, 2), 2)
    y = lax.div(me, 4)
    sib = me + 1 - 2 * core
    xn = me + 2 - 4 * x
    yn = me + 4 - 8 * y
    dn = xn + 4 - 8 * y
    xs, ys, ds = xn + 1 - 2 * core, yn + 1 - 2 * core, dn + 1 - 2 * core

    half, quarter = rows // 2, rows // 4
    lo, hi = (0, half), (half, half)
    lo_first, lo_second = (0, quarter), (quarter, quarter)

    def block(a, dp, zz, part=None):
        start, size = dp * rows, rows
        if part is not None:
            start, size = start + part[0], part[1]
        return full.at[
            a,
            pl.ds(pl.multiple_of(start, 16), size),
            pl.ds(pl.multiple_of(zz * width, 128), width),
        ]

    loads = [
        pltpu.make_async_copy(tok, block(0, me, z), load_sem.at[0]),
        pltpu.make_async_copy(cot, block(1, me, z), load_sem.at[1]),
        pltpu.make_async_copy(w_gate, wv.at[pl.ds(0, held)], load_sem.at[2]),
        pltpu.make_async_copy(w_up, wv.at[pl.ds(held, held)], load_sem.at[3]),
    ]
    for load in loads:
        load.start()

    barrier = pltpu.get_barrier_semaphore()
    for p in range(1, dp_count):
        pl.semaphore_signal(
            barrier, inc=1, device_id=(lax.rem(me + p, dp_count), z), device_id_type=MESH
        )

    @pl.when(z > 0)
    def _():
        pl.semaphore_signal(barrier, inc=1, device_id=(me, z - 1), device_id_type=MESH)

    @pl.when(z < depth - 1)
    def _():
        pl.semaphore_signal(barrier, inc=1, device_id=(me, z + 1), device_id_type=MESH)

    raw = weights[...]
    share = raw / jnp.sum(raw, axis=0, keepdims=True)
    named = ids[...]
    lines = [
        jnp.sum(jnp.where(named == e, share, 0.0), axis=0, keepdims=True) for e in range(experts)
    ]
    share_all[me] = jnp.concatenate(lines, axis=0)

    ends = jnp.where(z > 0, 1, 0) + jnp.where(z < depth - 1, 1, 0)
    pl.semaphore_wait(barrier, dp_count - 1 + ends)

    def place(k):
        a = lax.div(k, depth)
        s = k - a * depth
        m = jnp.minimum(z, depth - 1 - z)
        near = jnp.where(lax.rem(s, 2) == 1, z - lax.div(s + 1, 2), z + lax.div(s, 2))
        far = jnp.where(z == m, s, depth - 1 - s)
        zz = jnp.where(s <= 2 * m, near, far)
        return a, zz, a * depth + zz

    def remote(ref, r, kind, dp, zt, at=None):
        return pltpu.make_async_remote_copy(
            src_ref=ref,
            dst_ref=ref,
            send_sem=send_sem.at[r, kind],
            recv_sem=recv_sem.at[r, kind if at is None else at],
            device_id=(dp, zt),
            device_id_type=MESH,
        )

    def share_copy(p, dst):
        return pltpu.make_async_remote_copy(
            src_ref=share_all.at[me],
            dst_ref=share_all.at[me],
            send_sem=share_send.at[p],
            recv_sem=share_recv.at[p],
            device_id=(dst, z),
            device_id_type=MESH,
        )

    def line_block(k):
        a, zz, r = place(k)
        own = block(a, me, zz)

        @pl.when(zz != z)
        def _():
            remote(own, r, UP, me, z).wait_recv()

        @pl.when((zz <= z) & (z < depth - 1))
        def _():
            remote(own, r, UP, me, z + 1).start()

        @pl.when((zz >= z) & (z > 0))
        def _():
            remote(own, r, DOWN, me, z - 1, UP).start()

        remote(own, r, TO_X, xn, z).start()
        remote(own, r, TO_Y, yn, z).start()
        remote(own, r, TO_SIB, sib, z).start()

    def corner_start(a, zz, r, dp, kind, dst, near_part, far_part):
        @pl.when(zz == z)
        def _():
            remote(block(a, dp, zz, near_part), r, kind, dst, z).start()

        @pl.when(zz != z)
        def _():
            remote(block(a, dp, zz, far_part), r, kind, dst, z).start()

    def neighbour_blocks(k):
        a, zz, r = place(k)
        remote(block(a, xn, zz), r, TO_X, xn, z).wait_recv()
        corner_start(a, zz, r, xn, X_TO_Y, yn, lo, lo_first)
        remote(block(a, xn, zz), r, X_SIB, sib, z).start()
        remote(block(a, yn, zz), r, TO_Y, yn, z).wait_recv()
        corner_start(a, zz, r, yn, Y_TO_X, xn, hi, lo_second)
        remote(block(a, yn, zz), r, Y_SIB, sib, z).start()

    def diagonal_blocks(k):
        a, zz, r = place(k)

        @pl.when(zz == z)
        def _():
            remote(block(a, dn, zz, lo), r, X_TO_Y, yn, z).wait_recv()
            remote(block(a, dn, zz, hi), r, Y_TO_X, xn, z).wait_recv()

        @pl.when(zz != z)
        def _():
            remote(block(a, dn, zz, hi), r, DZ_UP, me, z).wait_recv()

        corner = block(a, dn, zz, hi)

        @pl.when((zz <= z) & (z < depth - 1))
        def _():
            remote(corner, r, DZ_UP, me, z + 1).start()

        @pl.when((zz >= z) & (z > 0))
        def _():
            remote(corner, r, DZ_DOWN, me, z - 1, DZ_UP).start()

        remote(corner, r, D_HI, sib, z).start()

        @pl.when(zz != z)
        def _():
            remote(block(a, dn, zz, lo_first), r, X_TO_Y, yn, z).wait_recv()
            remote(block(a, dn, zz, lo_second), r, Y_TO_X, xn, z).wait_recv()

        remote(block(a, dn, zz, lo), r, D_LO, sib, z).start()

    def sibling_blocks(k):
        a, zz, r = place(k)
        remote(block(a, sib, zz), r, TO_SIB, sib, z).wait_recv()
        remote(block(a, xs, zz), r, X_SIB, sib, z).wait_recv()
        remote(block(a, ys, zz), r, Y_SIB, sib, z).wait_recv()
        remote(block(a, ds, zz, lo), r, D_LO, sib, z).wait_recv()
        remote(block(a, ds, zz, hi), r, D_HI, sib, z).wait_recv()

    def sent(k):
        a, zz, r = place(k)
        own = block(a, me, zz)

        @pl.when((zz <= z) & (z < depth - 1))
        def _():
            remote(own, r, UP, me, z + 1).wait_send()

        @pl.when((zz >= z) & (z > 0))
        def _():
            remote(own, r, DOWN, me, z - 1, UP).wait_send()

        remote(own, r, TO_X, xn, z).wait_send()
        remote(own, r, TO_Y, yn, z).wait_send()
        remote(own, r, TO_SIB, sib, z).wait_send()
        remote(block(a, xn, zz), r, X_SIB, sib, z).wait_send()
        remote(block(a, yn, zz), r, Y_SIB, sib, z).wait_send()
        remote(block(a, dn, zz, lo), r, D_LO, sib, z).wait_send()
        corner = block(a, dn, zz, hi)
        remote(corner, r, D_HI, sib, z).wait_send()

        @pl.when(zz == z)
        def _():
            remote(block(a, xn, zz, lo), r, X_TO_Y, yn, z).wait_send()
            remote(block(a, yn, zz, hi), r, Y_TO_X, xn, z).wait_send()

        @pl.when(zz != z)
        def _():
            remote(block(a, xn, zz, lo_first), r, X_TO_Y, yn, z).wait_send()
            remote(block(a, yn, zz, lo_second), r, Y_TO_X, xn, z).wait_send()

        @pl.when((zz <= z) & (z < depth - 1))
        def _():
            remote(corner, r, DZ_UP, me, z + 1).wait_send()

        @pl.when((zz >= z) & (z > 0))
        def _():
            remote(corner, r, DZ_DOWN, me, z - 1, DZ_UP).wait_send()

    tile = math.gcd(total, width)

    def project(k):
        _, zz, _ = place(k)
        cols = pl.ds(pl.multiple_of(zz * width, 128), width)
        for g in range(2):
            @pl.loop(0, total // tile)
            def _(i):
                at = pl.ds(pl.multiple_of(i * tile, tile), tile)
                part = lax.dot_general(
                    wv[pl.ds(g * held, held), cols],
                    full[0, at, cols],
                    (((1,), (1,)), ((), ())),
                    preferred_element_type=jnp.float32,
                )

                @pl.when(k == 0)
                def _():
                    acc[pl.ds(g * held, held), at] = part

                @pl.when(k > 0)
                def _():
                    acc[pl.ds(g * held, held), at] += part

    def activate():
        for p in range(1, dp_count):
            src = lax.rem(me + dp_count - p, dp_count)
            pltpu.make_async_remote_copy(
                src_ref=share_all.at[src],
                dst_ref=share_all.at[src],
                send_sem=share_send.at[p],
                recv_sem=share_recv.at[p],
                device_id=(src, z),
                device_id_type=MESH,
            ).wait_recv()

        @pl.loop(0, dp_count)
        def _(p):
            at = pl.ds(pl.multiple_of(p * rows, 128), rows)
            for e in range(exp_dev):
                gate = acc[pl.ds(e * hidden, hidden), at]
                up = acc[pl.ds(held + e * hidden, hidden), at]
                line = share_all[p, pl.ds(me * exp_dev + e, 1), :]
                value = gate / (1.0 + jnp.exp(-gate)) * up * line
                hid[pl.ds(e * hidden, hidden), at] = value.astype(hid.dtype)

    def store(k):
        _, zz, _ = place(k)
        cols = pl.ds(pl.multiple_of(zz * width, 128), width)
        return pltpu.make_async_copy(obuf.at[:, cols], out.at[:, cols], out_sem.at[zz])

    def down(k):
        _, zz, _ = place(k)

        @pl.loop(0, width // tile)
        def _(i):
            at = pl.ds(pl.multiple_of(zz * width + i * tile, tile), tile)
            obuf[:, at] = jnp.dot(
                hid[...], full[1, :, at], preferred_element_type=jnp.float32
            ).astype(obuf.dtype)

        store(k).start()

    loads[0].wait()
    loads[1].wait()
    line_block(0)
    for p in range(1, dp_count):
        share_copy(p, lax.rem(me + p, dp_count)).start()
    line_block(1)
    neighbour_blocks(0)
    line_block(2)
    neighbour_blocks(1)
    diagonal_blocks(0)
    loads[2].wait()
    loads[3].wait()

    @pl.loop(0, steps)
    def _(k):
        @pl.when(k + 3 < steps)
        def _():
            line_block(k + 3)

        @pl.when(k + 2 < steps)
        def _():
            neighbour_blocks(k + 2)

        @pl.when(k + 1 < steps)
        def _():
            diagonal_blocks(k + 1)

        sibling_blocks(k)

        @pl.when(k < depth)
        def _():
            project(k)

        @pl.when(k == depth - 1)
        def _():
            activate()

        @pl.when(k >= depth)
        def _():
            down(k)

    @pl.loop(0, steps)
    def _(k):
        sent(k)

    for p in range(1, dp_count):
        share_copy(p, lax.rem(me + p, dp_count)).wait_send()

    @pl.loop(depth, steps)
    def _(k):
        store(k).wait()


def scratch_bytes(dp_count, depth, rows, width, exp_dev, hidden):
    total, model, held = dp_count * rows, depth * width, exp_dev * hidden
    return 4 * total * model + 4 * held * model + 8 * held * total + 2 * held * (total + model)


def gather_plan(sizes, tokens, cotangent, expert_ids, route_weights, w_gate, w_up):
    dp_count, depth, rows, width, exp_dev, hidden = sizes
    total, model, held = dp_count * rows, depth * width, exp_dev * hidden
    experts = exp_dev * dp_count
    steps = 2 * depth
    hbm = pl.BlockSpec(memory_space=pl.ANY)
    vmem = pl.BlockSpec(memory_space=pltpu.VMEM)
    grad = pl.pallas_call(
        functools.partial(gather_kernel, sizes),
        out_shape=jax.ShapeDtypeStruct((held, model), jnp.bfloat16),
        in_specs=[hbm, hbm, vmem, vmem, hbm, hbm],
        out_specs=hbm,
        scratch_shapes=[
            pltpu.VMEM((2, total, model), jnp.bfloat16),
            pltpu.VMEM((2 * held, model), jnp.bfloat16),
            pltpu.VMEM((2 * held, total), jnp.float32),
            pltpu.VMEM((held, total), jnp.bfloat16),
            pltpu.VMEM((held, model), jnp.bfloat16),
            pltpu.VMEM((dp_count, experts, rows), jnp.float32),
            pltpu.SemaphoreType.DMA((steps, KINDS)),
            pltpu.SemaphoreType.DMA((steps, KINDS)),
            pltpu.SemaphoreType.DMA((dp_count,)),
            pltpu.SemaphoreType.DMA((dp_count,)),
            pltpu.SemaphoreType.DMA((4,)),
            pltpu.SemaphoreType.DMA((depth,)),
        ],
        compiler_params=pltpu.CompilerParams(
            collective_id=0, has_side_effects=True, vmem_limit_bytes=VMEM_BUDGET
        ),
        cost_estimate=pl.CostEstimate(
            flops=6 * held * total * model,
            bytes_accessed=6 * held * model + 4 * rows * width,
            transcendentals=held * total,
        ),
    )(
        tokens,
        cotangent,
        expert_ids.T,
        route_weights.T,
        w_gate.reshape(held, model),
        w_up.reshape(held, model),
    )
    return grad.reshape(exp_dev, hidden, model)


def build_table(flat_ids, first_expert, held_count, block_count, capacity):
    local_expert = flat_ids - first_expert
    inside = (local_expert >= 0) & (local_expert < held_count)
    onehot = (local_expert[:, :, None] == jnp.arange(held_count)[None, None, :]).astype(jnp.int32)
    slot_index = jnp.sum((jnp.cumsum(onehot, axis=1) - 1) * onehot, axis=2)
    block_index = jnp.arange(block_count)[:, None]
    target = local_expert * (block_count * capacity) + block_index * capacity + slot_index
    target = jnp.where(inside, target, held_count * block_count * capacity)
    pair_index = jnp.arange(flat_ids.shape[0] * flat_ids.shape[1])
    empty_table = jnp.full((held_count * block_count * capacity,), -1, jnp.int32)
    return empty_table.at[target.reshape(-1)].set(pair_index, mode="drop")


def pick_rows(slot_table, token_rows, cot_rows, flat_shares, top_count):
    is_live = slot_table >= 0
    safe_index = jnp.maximum(slot_table, 0)
    token_row = safe_index // top_count
    routed = jnp.where(is_live[:, None], token_rows[token_row], jnp.zeros((), token_rows.dtype))
    weighting = jnp.where(is_live, flat_shares[safe_index], 0.0)
    scaled_rows = (weighting[:, None] * cot_rows[token_row].astype(jnp.float32)).astype(
        jnp.bfloat16
    )
    return (routed, scaled_rows)


def routed_plan(tokens, cotangent, expert_ids, route_weights, w_gate, w_up):
    dp_count = lax.axis_size("dp")
    exp_dev = w_gate.shape[0]
    experts = exp_dev * dp_count
    tok_rows, width_local = tokens.shape
    top_count = expert_ids.shape[1]
    capacity = 3 * tok_rows * top_count // (2 * experts)
    shares = route_weights / jnp.sum(route_weights, axis=1, keepdims=True)
    slot_table = build_table(expert_ids.reshape(1, tok_rows * top_count), 0, experts, 1, capacity)
    routed, scaled_rows = pick_rows(slot_table, tokens, cotangent, shares.reshape(-1), top_count)
    send_rows = routed.reshape(experts, capacity, width_local)
    send_cot = scaled_rows.reshape(experts, capacity, width_local)
    wide_rows = lax.all_gather(send_rows, "tensor", axis=2, tiled=True)
    received, cot_recv = (
        lax.all_to_all(wide_rows, "dp", split_axis=0, concat_axis=1, tiled=True),
        lax.all_to_all(send_cot, "dp", split_axis=0, concat_axis=1, tiled=True),
    )
    gate_proj = jnp.einsum("erd,efd->erf", received, w_gate, preferred_element_type=jnp.float32)
    up_proj = jnp.einsum("erd,efd->erf", received, w_up, preferred_element_type=jnp.float32)
    hidden = (jax.nn.silu(gate_proj) * up_proj).astype(jnp.bfloat16)
    return jnp.einsum(
        "erf,erd->efd",
        hidden,
        lax.all_gather(cot_recv, "tensor", axis=2, tiled=True),
        preferred_element_type=jnp.float32,
    ).astype(jnp.bfloat16)


def shards(tokens, cotangent, expert_ids, route_weights, w_gate, w_up):
    dp_count, depth = lax.axis_size("dp"), lax.axis_size("tensor")
    sizes = (dp_count, depth) + tokens.shape + w_gate.shape[:2]
    if dp_count == 8 and scratch_bytes(*sizes) < VMEM_BUDGET * 9 // 10:
        return gather_plan(sizes, tokens, cotangent, expert_ids, route_weights, w_gate, w_up)
    return routed_plan(tokens, cotangent, expert_ids, route_weights, w_gate, w_up)


def solution(mesh):
    placed = (
        P("dp", "tensor"),
        P("dp", "tensor"),
        P("dp", None),
        P("dp", None),
        P("dp", "tensor", None),
        P("dp", "tensor", None),
    )
    return jax.shard_map(
        shards, mesh=mesh, in_specs=placed, out_specs=P("dp", "tensor", None), check_vma=False
    )
```
